32 devices in a mesh: ctx: 8 (over y, x, core), tp: 4 (over z).
Axes of the slice: x: 2, y: 2, z: 4, core: 2. Of those that a mesh axis runs over, the one named last changes fastest.
Arguments:
- queries: bfloat16 [2048, 64, 128], P('ctx', 'tp'), may hold values from -24 to 24
- keys: bfloat16 [2048, 8, 128], P('ctx', 'tp'), may hold values from -24 to 24
- values: bfloat16 [2048, 8, 128], P('ctx', 'tp'), may hold values from -6 to 6
- positions: int32 [2048], replicated, may hold values from 0 to 2047, as said below
- out_weight: bfloat16 [8192, 8192], P('tp'), may hold values from -0.0625 to 0.0625
- grad_out: bfloat16 [2048, 8192], P('ctx'), may hold values from -6 to 6
Outputs:
- layer_out: bfloat16 [2048, 8192], P('ctx', 'tp')
- grad_queries: bfloat16 [2048, 64, 128], P('ctx', 'tp')
- grad_keys: bfloat16 [2048, 8, 128], P('ctx', 'tp')
- grad_values: bfloat16 [2048, 8, 128], P('ctx', 'tp')
The draws below stay inside these ranges and needn't reach their ends.
Inputs may be any that keep to these rules, and one draw needn't show every extreme that they name: positions is a permutation of 0 to 2047. The rows of each index of ctx (256 rows) hold two whole blocks of 128 consecutive positions in rising order: block numbers b and 15 - b, in either order; which b a device holds is drawn.
All inputs are finite; a program needn't handle non-finite values.
Results may differ from the reference program's by a relative error of at most 0.035.
Values may be sent and summed in bfloat16 or wider, within the bound.
A program may use at most 128 MiB of HBM per device.

```python
import math
import jax
import jax.numpy as jnp
from jax import lax

H = 64
KVH = 8
HD = 128
D = 8192
SPAN = 128
SEQ = 2048
N_TP = 4


def draw_queries(key, part):
    key = jax.random.fold_in(key, 11)
    drawn = jax.random.normal(key, (SEQ, H, HD), jnp.float32)
    return jnp.clip(drawn, -24.0, 24.0).astype(jnp.bfloat16)


def draw_keys(key, part):
    key = jax.random.fold_in(key, 13)
    drawn = jax.random.normal(key, (SEQ, KVH, HD), jnp.float32)
    return jnp.clip(drawn, -24.0, 24.0).astype(jnp.bfloat16)


def draw_positions(key, part):
    key = jax.random.fold_in(key, 29)
    pair_count = SEQ // (2 * SPAN)
    pair_order = jax.random.permutation(key, pair_count)
    flipped = jax.random.randint(jax.random.fold_in(key, 1), (pair_count,), 0, 2)
    mirror = 2 * pair_count - 1 - pair_order
    first_block = jnp.where(flipped == 1, mirror, pair_order)
    second_block = jnp.where(flipped == 1, pair_order, mirror)
    block_ids = jnp.stack([first_block, second_block], axis=1)
    position_grid = block_ids[:, :, None] * SPAN + jnp.arange(SPAN)[None, None, :]
    return position_grid.reshape(SEQ).astype(jnp.int32)


def block_scale(own_key, shape, shards, least, high):
    def one(dim, blocks):
        draws = jax.random.uniform(jax.random.fold_in(jax.random.fold_in(own_key, 6), dim), (blocks,), jnp.float32, least / len(shards), high / len(shards))
        return jnp.repeat(jnp.exp(draws), shape[dim] // blocks).reshape((-1,) + (1,) * (len(shape) - dim - 1))

    level = one(*shards[0])
    for cut in shards[1:]:
        level = level * one(*cut)
    return level


def centred(key, extent, scale, bound, split=(), kind=jnp.bfloat16):
    array = jax.random.normal(key, extent, jnp.float32) * scale
    if len(split) > 0:
        array = block_scale(key, extent, split, -0.22, 0.18) * array
    return jnp.clip(array, min=-bound, max=bound).astype(kind)


def setup_inputs(seed: int = 0) -> dict:
    seeds = jax.random.split(jax.random.key(seed), 7)
    return {
        "queries": draw_queries(jax.random.fold_in(seeds[6], 71), 0),
        "keys": draw_keys(jax.random.fold_in(seeds[6], 71), 0),
        "values": centred(seeds[2], (SEQ, KVH, HD), 1.0, 6.0, ((0, 8), (1, 4))),
        "positions": draw_positions(jax.random.fold_in(seeds[6], 71), 0),
        "out_weight": centred(seeds[4], (H * HD, D), (H * HD) ** -0.5, 0.0625, ((0, 4),)),
        "grad_out": centred(seeds[5], (SEQ, D), 1.0, 6.0, ((0, 8),)),
    }


NEG_FILL = -1e+30

def heads_first(array_in):
    return jnp.transpose(array_in, (1, 0, 2))

def reference(queries, keys, values, positions, out_weight, grad_out):
    group_size = H // KVH
    score_scale = 1.0 / math.sqrt(HD)
    allowed = positions[None, :] <= positions[:, None]
    grad_heads = jnp.dot(grad_out, out_weight.T, preferred_element_type=jnp.float32).astype(jnp.bfloat16)
    grad_heads = grad_heads.reshape(SEQ, H, HD)

    def one_head(operands):
        query_head, key_head, value_head, grad_head = operands
        scores = jnp.dot(query_head, key_head.T, preferred_element_type=jnp.float32) * score_scale
        scores = jnp.where(allowed, scores, NEG_FILL)
        top_score = lax.optimization_barrier(jnp.max(scores, axis=1))
        log_total = top_score + jnp.log(lax.optimization_barrier(jnp.sum(jnp.exp(scores - top_score[:, None]), axis=1)))
        weights = jnp.exp(scores - log_total[:, None])
        weights_bf = weights.astype(jnp.bfloat16)
        attended = jnp.dot(weights_bf, value_head, preferred_element_type=jnp.float32).astype(jnp.bfloat16)
        row_delta = lax.optimization_barrier(jnp.sum(attended.astype(jnp.float32) * grad_head.astype(jnp.float32), axis=1))
        dweights = jnp.dot(grad_head, value_head.T, preferred_element_type=jnp.float32)
        dscores = (weights * (dweights - row_delta[:, None])).astype(jnp.bfloat16)
        grad_query = (jnp.dot(dscores, key_head, preferred_element_type=jnp.float32) * score_scale).astype(jnp.bfloat16)
        grad_key = jnp.dot(dscores.T, query_head, preferred_element_type=jnp.float32) * score_scale
        grad_value = jnp.dot(weights_bf.T, grad_head, preferred_element_type=jnp.float32)
        return (attended, grad_query, grad_key, grad_value)
    key_heads = jnp.repeat(heads_first(keys), group_size, axis=0)
    value_heads = jnp.repeat(heads_first(values), group_size, axis=0)
    attended, grad_query, grad_key, grad_value = lax.map(one_head, (heads_first(queries), key_heads, value_heads, heads_first(grad_heads)))
    grad_key = lax.optimization_barrier(jnp.sum(grad_key.reshape(KVH, group_size, SEQ, HD), axis=1))
    grad_value = lax.optimization_barrier(jnp.sum(grad_value.reshape(KVH, group_size, SEQ, HD), axis=1))
    flat = heads_first(attended).reshape(SEQ, N_TP, H // N_TP * HD)
    weight_parts = out_weight.reshape(N_TP, H // N_TP * HD, D)

    def add_part(total_now, index_now):
        part_rows = lax.dynamic_index_in_dim(flat, index_now, 1, keepdims=False)
        part_weight = lax.dynamic_index_in_dim(weight_parts, index_now, 0, keepdims=False)
        part_now = jnp.dot(part_rows, part_weight, preferred_element_type=jnp.float32).astype(jnp.bfloat16)
        part_now = lax.optimization_barrier(part_now)
        return (total_now + part_now.astype(jnp.float32), None)
    summed, _ = lax.scan(add_part, jnp.zeros((SEQ, D), jnp.float32), jnp.arange(N_TP, dtype=jnp.int32))
    layer_out = summed.astype(jnp.bfloat16)
    return (layer_out, heads_first(grad_query), heads_first(grad_key).astype(jnp.bfloat16), heads_first(grad_value).astype(jnp.bfloat16))
```

```python
import functools
import math

import jax
import jax.numpy as jnp
from jax import lax
from jax.experimental import pallas as pl
from jax.experimental.pallas import tpu as pltpu
from jax.sharding import PartitionSpec as P

NEG_FILL = -1e30
LOG2E = 1.4426950408889634
PAIR = 256
COLS = 256
F32 = jnp.float32
BF16 = jnp.bfloat16
VMEM_LIMIT = 50 * 1024 * 1024


def dot(a, b):
    return jnp.dot(a, b, preferred_element_type=F32)


def scores_t(k_tile, qt_part, scale):
    return dot(k_tile, qt_part) * scale


def mask_t(scores, key_start, query_start, span):
    key_pos = key_start + lax.broadcasted_iota(jnp.int32, scores.shape, 0)
    query_pos = query_start + lax.broadcasted_iota(jnp.int32, scores.shape, 1) % span
    return jnp.where(key_pos <= query_pos, scores, NEG_FILL)


def load_sorted(info_ref, src_ref, blocks, span):
    for j in range(blocks):
        stored = info_ref[j]
        yield j, src_ref[stored // 2, 0, stored % 2]


def forward_kernel(blocks, span, scale, info_ref, q_ref, k_ref, v_ref, att_ref, att_t_ref, lse_ref,
                   k_sorted, v_t, q_t, out_t, top, total):
    half = pl.program_id(1)
    heads = q_ref.shape[1] // span
    query_block = info_ref[blocks + half]

    @pl.when(half == 0)
    def _():
        for j, block in load_sorted(info_ref, k_ref, blocks, span):
            k_sorted[j * span:(j + 1) * span, :] = block
        for j, block in load_sorted(info_ref, v_ref, blocks, span):
            v_t[:, j * span:(j + 1) * span] = block.T

    for h in range(heads):
        q_t[:, h * span:(h + 1) * span] = q_ref[:, h * span:(h + 1) * span].T
    out_t[...] = jnp.zeros_like(out_t)
    top[...] = jnp.full_like(top, NEG_FILL)
    total[...] = jnp.zeros_like(total)

    def step(j, masked):
        start = pl.multiple_of(j * PAIR, PAIR)
        k_tile = k_sorted[pl.ds(start, PAIR), :]
        v_tile = v_t[:, pl.ds(start, PAIR)]
        for c in range(0, q_t.shape[1], COLS):
            cols = slice(c, c + COLS)
            scores = scores_t(k_tile, q_t[:, cols], scale)
            if masked:
                scores = mask_t(scores, start, query_block * span, span)
            old_top = top[:, cols]
            new_top = jnp.maximum(old_top, jnp.max(scores, axis=0, keepdims=True))
            weights = jnp.exp2(scores - new_top)
            factor = jnp.exp2(old_top - new_top)
            top[:, cols] = new_top
            total[:, cols] = total[:, cols] * factor + jnp.sum(weights, axis=0, keepdims=True)
            out_t[:, cols] = out_t[:, cols] * factor + dot(v_tile, weights.astype(BF16))

    last = query_block // 2
    pl.loop(0, last)(lambda j: step(j, False))
    step(last, True)

    lse_ref[0, 0] = top[...] + jnp.log2(total[...])
    inverse = 1.0 / total[...]
    for h in range(heads):
        cols = slice(h * span, (h + 1) * span)
        part = out_t[:, cols] * inverse[:, cols]
        att_t_ref[0, 0, :, cols] = part.astype(BF16)
        att_ref[:, cols] = part.T.astype(BF16)


def backward_kernel(blocks, span, scale, out_scale, info_ref, q_ref, go_ref, k_ref, v_ref, att_t_ref,
                    lse_ref, gq_ref, gkv_ref, k_sorted, v_sorted, k_t, q_s, q_t, go_s, go_t, gq_t,
                    delta, gk, gv):
    half = pl.program_id(0)
    heads = q_ref.shape[1] // span
    query_block = info_ref[blocks + half]

    @pl.when(half == 0)
    def _():
        for j, block in load_sorted(info_ref, k_ref, blocks, span):
            k_sorted[j * span:(j + 1) * span, :] = block
            k_t[:, j * span:(j + 1) * span] = block.T
        for j, block in load_sorted(info_ref, v_ref, blocks, span):
            v_sorted[j * span:(j + 1) * span, :] = block
        gk[...] = jnp.zeros_like(gk)
        gv[...] = jnp.zeros_like(gv)

    for h in range(heads):
        part = slice(h * span, (h + 1) * span)
        q_s[part, :] = q_ref[:, part]
        q_t[:, part] = q_ref[:, part].T
        go_s[part, :] = go_ref[:, part]
        turned = go_ref[:, part].T
        go_t[:, part] = turned
        delta[:, part] = jnp.sum(
            att_t_ref[0, 0, :, part].astype(F32) * turned.astype(F32), axis=0, keepdims=True
        )
    gq_t[...] = jnp.zeros_like(gq_t)

    def step(j, masked):
        start = pl.multiple_of(j * PAIR, PAIR)
        rows = pl.ds(start, PAIR)
        k_tile = k_sorted[rows, :]
        v_tile = v_sorted[rows, :]
        kt_tile = k_t[:, rows]
        all_w, all_d = [], []
        for c in range(0, q_t.shape[1], COLS):
            cols = slice(c, c + COLS)
            scores = scores_t(k_tile, q_t[:, cols], scale)
            if masked:
                scores = mask_t(scores, start, query_block * span, span)
            weights = jnp.exp2(scores - lse_ref[0, 0, :, cols])
            dweights = dot(v_tile, go_t[:, cols])
            dscores = (weights * (dweights - delta[:, cols])).astype(BF16)
            gq_t[:, cols] += dot(kt_tile, dscores)
            all_w.append(weights.astype(BF16))
            all_d.append(dscores)
        gv[rows, :] += dot(jnp.concatenate(all_w, axis=1), go_s[...])
        gk[rows, :] += dot(jnp.concatenate(all_d, axis=1), q_s[...])

    last = query_block // 2
    pl.loop(0, last)(lambda j: step(j, False))
    step(last, True)

    for h in range(heads):
        part = slice(h * span, (h + 1) * span)
        gq_ref[:, part] = (gq_t[:, part] * out_scale).T.astype(BF16)

    @pl.when(half == 1)
    def _():
        for j in range(blocks):
            stored = info_ref[j]
            part = slice(j * span, (j + 1) * span)
            gkv_ref[stored // 2, 0, stored % 2] = (gk[part, :] * out_scale).astype(BF16)
            gkv_ref[stored // 2, 1, stored % 2] = gv[part, :].astype(BF16)


def project_kernel(info_ref, a_ref, w_ref, o_ref):
    o_ref[...] = dot(a_ref[...], w_ref[...]).astype(BF16)


def project(first, attended, weight, width):
    rows, depth = attended.shape
    tile = 512
    return pl.pallas_call(
        project_kernel,
        out_shape=jax.ShapeDtypeStruct((rows, width), BF16),
        grid_spec=pltpu.PrefetchScalarGridSpec(
            num_scalar_prefetch=1,
            grid=(width // tile,),
            in_specs=[
                pl.BlockSpec((rows, depth), lambda i, info: (0, 0)),
                pl.BlockSpec((depth, tile), lambda i, info: (0, info[0] * (width // tile) + i)),
            ],
            out_specs=pl.BlockSpec((rows, tile), lambda i, info: (0, i)),
        ),
        compiler_params=pltpu.CompilerParams(vmem_limit_bytes=VMEM_LIMIT),
        cost_estimate=pl.CostEstimate(
            flops=2 * rows * depth * width, bytes_accessed=2 * depth * width, transcendentals=0
        ),
    )(first, attended, weight)


def forward(info, q2, kv_all, span):
    rows, flat = q2.shape
    ctx, kv2, _, _, hd = kv_all.shape
    kvl = kv2 // 2
    blocks = ctx * 2
    seq = blocks * span
    width = flat // kvl
    kernel = functools.partial(forward_kernel, blocks, span, LOG2E / math.sqrt(hd))
    work = rows * seq * flat // 2
    return pl.pallas_call(
        kernel,
        out_shape=(
            jax.ShapeDtypeStruct((rows, flat), BF16),
            jax.ShapeDtypeStruct((kvl, 2, hd, width), BF16),
            jax.ShapeDtypeStruct((kvl, 2, 1, width), F32),
        ),
        grid_spec=pltpu.PrefetchScalarGridSpec(
            num_scalar_prefetch=1,
            grid=(kvl, 2),
            in_specs=[
                pl.BlockSpec((span, width), lambda g, i, info: (i, g)),
                pl.BlockSpec((ctx, 1, 2, span, hd), lambda g, i, info: (0, g, 0, 0, 0)),
                pl.BlockSpec((ctx, 1, 2, span, hd), lambda g, i, info: (0, kvl + g, 0, 0, 0)),
            ],
            out_specs=(
                pl.BlockSpec((span, width), lambda g, i, info: (i, g)),
                pl.BlockSpec((1, 1, hd, width), lambda g, i, info: (g, i, 0, 0)),
                pl.BlockSpec((1, 1, 1, width), lambda g, i, info: (g, i, 0, 0)),
            ),
            scratch_shapes=[
                pltpu.VMEM((seq, hd), BF16),
                pltpu.VMEM((hd, seq), BF16),
                pltpu.VMEM((hd, width), BF16),
                pltpu.VMEM((hd, width), F32),
                pltpu.VMEM((1, width), F32),
                pltpu.VMEM((1, width), F32),
            ],
        ),
        compiler_params=pltpu.CompilerParams(vmem_limit_bytes=VMEM_LIMIT),
        cost_estimate=pl.CostEstimate(
            flops=8 * work, bytes_accessed=4 * rows * flat, transcendentals=work // hd
        ),
    )(info, q2, kv_all, kv_all)


def backward(info, q2, go2, kv_all, att_t, lse, span, g):
    rows, flat = q2.shape
    ctx, kv2, _, _, hd = kv_all.shape
    kvl = kv2 // 2
    blocks = ctx * 2
    seq = blocks * span
    width = flat // kvl
    kernel = functools.partial(
        backward_kernel, blocks, span, LOG2E / math.sqrt(hd), 1.0 / math.sqrt(hd)
    )
    work = rows * seq * width // 2
    return pl.pallas_call(
        kernel,
        out_shape=(
            jax.ShapeDtypeStruct((rows, width), BF16),
            jax.ShapeDtypeStruct((ctx, 2, 2, span, hd), BF16),
        ),
        grid_spec=pltpu.PrefetchScalarGridSpec(
            num_scalar_prefetch=1,
            grid=(2,),
            in_specs=[
                pl.BlockSpec((span, width), lambda i, info: (i, g)),
                pl.BlockSpec((span, width), lambda i, info: (i, g)),
                pl.BlockSpec((ctx, 1, 2, span, hd), lambda i, info: (0, g, 0, 0, 0)),
                pl.BlockSpec((ctx, 1, 2, span, hd), lambda i, info: (0, kvl + g, 0, 0, 0)),
                pl.BlockSpec((1, 1, hd, width), lambda i, info: (g, i, 0, 0)),
                pl.BlockSpec((1, 1, 1, width), lambda i, info: (g, i, 0, 0)),
            ],
            out_specs=(
                pl.BlockSpec((span, width), lambda i, info: (i, 0)),
                pl.BlockSpec((ctx, 2, 2, span, hd), lambda i, info: (0, 0, 0, 0, 0)),
            ),
            scratch_shapes=[
                pltpu.VMEM((seq, hd), BF16),
                pltpu.VMEM((seq, hd), BF16),
                pltpu.VMEM((hd, seq), BF16),
                pltpu.VMEM((width, hd), BF16),
                pltpu.VMEM((hd, width), BF16),
                pltpu.VMEM((width, hd), BF16),
                pltpu.VMEM((hd, width), BF16),
                pltpu.VMEM((hd, width), F32),
                pltpu.VMEM((1, width), F32),
                pltpu.VMEM((seq, hd), F32),
                pltpu.VMEM((seq, hd), F32),
            ],
        ),
        compiler_params=pltpu.CompilerParams(vmem_limit_bytes=VMEM_LIMIT),
        cost_estimate=pl.CostEstimate(
            flops=20 * work, bytes_accessed=4 * rows * flat, transcendentals=work // hd
        ),
    )(info, q2, go2, kv_all, kv_all, att_t, lse)


def local(queries, keys, values, positions, out_weight, grad_out):
    rows, heads, hd = queries.shape
    kvl = keys.shape[1]
    span = rows // 2
    ctx = lax.axis_size("ctx")
    tp = lax.axis_size("tp")
    me = lax.axis_index("tp")
    seq = rows * ctx
    blocks = 2 * ctx
    model = out_weight.shape[1]
    chunk = model // tp

    kv = jnp.stack([keys, values]).transpose(0, 2, 1, 3).reshape(2 * kvl, 2, span, hd)
    kv_all = lax.all_gather(kv, "ctx", axis=0, tiled=False)

    block_of = positions.reshape(blocks, span)[:, 0] // span
    order = jnp.arange(blocks, dtype=jnp.int32)
    place = jnp.sum(jnp.where(block_of[None, :] == order[:, None], order[None, :], 0), axis=1)
    mine = lax.dynamic_slice_in_dim(block_of, 2 * lax.axis_index("ctx"), 2)
    info = jnp.concatenate([place, mine]).astype(jnp.int32)

    q2 = queries.reshape(rows, heads * hd)
    grad_heads = lax.dot_general(
        grad_out, out_weight, (((1,), (1,)), ((), ())), preferred_element_type=F32
    ).astype(BF16)

    attended, att_t, lse = forward(info, q2, kv_all, span)

    early = jnp.where(me < (tp + 1) // 2, tp - 1, 0).astype(jnp.int32).reshape(1)
    first = project(early, attended, out_weight, chunk)
    partial_out = project(jnp.zeros((1,), jnp.int32), attended, out_weight, model)

    def own_part(index):
        index = jnp.clip(index, 0, tp - 1)
        return lax.dynamic_slice_in_dim(partial_out, index * chunk, chunk, axis=1)

    right = left = first
    for k in range(tp - 1):
        to_right = [(z, z + 1) for z in range(tp - 1) if z <= k]
        to_left = [(tp - 1 - a, tp - 1 - b) for a, b in to_right]
        from_left = lax.ppermute(right, "tp", to_right).astype(F32)
        from_right = lax.ppermute(left, "tp", to_left).astype(F32)
        if k < tp - 2:
            right = (own_part(tp - 2 - k + me).astype(F32) + from_left).astype(BF16)
            left = (own_part(k + 2 - tp + me).astype(F32) + from_right).astype(BF16)
    layer_out = (own_part(me).astype(F32) + from_left + from_right).astype(BF16)

    query_parts, kv_parts = [], []
    for g in range(kvl):
        gq, gkv = backward(info, q2, grad_heads, kv_all, att_t, lse, span, g)
        query_parts.append(gq)
        kv_parts.append(gkv)
    grad_queries = jnp.concatenate(query_parts, axis=1).reshape(rows, heads, hd)
    terms = jnp.stack(kv_parts, axis=1).reshape(ctx, kvl, 2, rows, hd)
    owned = lax.psum_scatter(terms, "ctx", scatter_dimension=0, tiled=False)
    return (
        layer_out,
        grad_queries,
        owned[:, 0].transpose(1, 0, 2),
        owned[:, 1].transpose(1, 0, 2),
    )


def solution(mesh):
    placed = (
        P("ctx", "tp", None),
        P("ctx", "tp", None),
        P("ctx", "tp", None),
        P(),
        P("tp", None),
        P("ctx", None),
    )
    return jax.shard_map(
        local,
        mesh=mesh,
        in_specs=placed,
        out_specs=(
            P("ctx", "tp"),
            P("ctx", "tp", None),
            P("ctx", "tp", None),
            P("ctx", "tp", None),
        ),
        check_vma=False,
    )
```

```python
import functools
import math

import jax
import jax.numpy as jnp
from jax import lax
from jax.experimental import pallas as pl
from jax.experimental.pallas import tpu as pltpu
from jax.sharding import PartitionSpec as P

NEG_FILL = -1e30
LOG2E = 1.4426950408889634
PAIR = 256
FORWARD_COLS = 512
BACKWARD_COLS = 256
F32 = jnp.float32
BF16 = jnp.bfloat16
VMEM_LIMIT = 50 * 1024 * 1024


def dot(a, b):
    return jnp.dot(a, b, preferred_element_type=F32)


def mask_t(scores, key_start, query_start, span):
    key_pos = key_start + lax.broadcasted_iota(jnp.int32, scores.shape, 0)
    query_pos = query_start + lax.broadcasted_iota(jnp.int32, scores.shape, 1) % span
    return jnp.where(key_pos <= query_pos, scores, NEG_FILL)


def in_turn(count, multiply, weigh, collect):
    for n in range(count + 2):
        if n < count:
            multiply(n)
        if 1 <= n <= count:
            weigh(n - 1)
        if n >= 2:
            collect(n - 2)


def load_sorted(info_ref, src_ref, blocks, span):
    for j in range(blocks):
        stored = info_ref[j]
        yield j, src_ref[stored // 2, 0, stored % 2]


def forward_kernel(blocks, span, scale, info_ref, q_ref, k_ref, v_ref, att_ref, att_t_ref, lse_ref,
                   k_sorted, v_t, q_t, out_t, top, total):
    half = pl.program_id(1)
    heads = q_ref.shape[1] // span
    query_block = info_ref[blocks + half]

    @pl.when(half == 0)
    def _():
        for j, block in load_sorted(info_ref, k_ref, blocks, span):
            k_sorted[j * span:(j + 1) * span, :] = block
        for j, block in load_sorted(info_ref, v_ref, blocks, span):
            v_t[:, j * span:(j + 1) * span] = block.T

    for h in range(heads):
        q_t[:, h * span:(h + 1) * span] = q_ref[:, h * span:(h + 1) * span].T
    out_t[...] = jnp.zeros_like(out_t)
    top[...] = jnp.full_like(top, NEG_FILL)
    total[...] = jnp.zeros_like(total)

    def step(j, masked):
        start = pl.multiple_of(j * PAIR, PAIR)
        k_tile = k_sorted[pl.ds(start, PAIR), :]
        v_tile = v_t[:, pl.ds(start, PAIR)]
        parts = [slice(c, c + FORWARD_COLS) for c in range(0, q_t.shape[1], FORWARD_COLS)]
        ready, weighted = {}, {}

        def multiply(n):
            ready[n] = dot(k_tile, q_t[:, parts[n]])

        def weigh(n):
            cols = parts[n]
            scores = ready.pop(n) * scale
            if masked:
                scores = mask_t(scores, start, query_block * span, span)
            old_top = top[:, cols]
            new_top = jnp.maximum(old_top, jnp.max(scores, axis=0, keepdims=True))
            weights = jnp.exp2(scores - new_top)
            factor = jnp.exp2(old_top - new_top)
            top[:, cols] = new_top
            total[:, cols] = total[:, cols] * factor + jnp.sum(weights, axis=0, keepdims=True)
            weighted[n] = (weights.astype(BF16), factor)

        def collect(n):
            weights, factor = weighted.pop(n)
            out_t[:, parts[n]] = out_t[:, parts[n]] * factor + dot(v_tile, weights)

        in_turn(len(parts), multiply, weigh, collect)

    last = query_block // 2
    pl.loop(0, last)(lambda j: step(j, False))
    step(last, True)

    lse_ref[0, 0] = top[...] + jnp.log2(total[...])
    inverse = 1.0 / total[...]
    for h in range(heads):
        cols = slice(h * span, (h + 1) * span)
        part = out_t[:, cols] * inverse[:, cols]
        att_t_ref[0, 0, :, cols] = part.astype(BF16)
        att_ref[:, cols] = part.T.astype(BF16)


def backward_kernel(blocks, span, scale, out_scale, info_ref, q_ref, go_ref, k_ref, v_ref, att_t_ref,
                    lse_ref, gq_ref, gkv_ref, k_sorted, v_sorted, k_t, q_s, q_t, go_s, go_t, gq_t,
                    delta, gk, gv):
    half = pl.program_id(0)
    heads = q_ref.shape[1] // span
    query_block = info_ref[blocks + half]

    @pl.when(half == 0)
    def _():
        for j, block in load_sorted(info_ref, k_ref, blocks, span):
            k_sorted[j * span:(j + 1) * span, :] = block
            k_t[:, j * span:(j + 1) * span] = block.T
        for j, block in load_sorted(info_ref, v_ref, blocks, span):
            v_sorted[j * span:(j + 1) * span, :] = block
        gk[...] = jnp.zeros_like(gk)
        gv[...] = jnp.zeros_like(gv)

    for h in range(heads):
        part = slice(h * span, (h + 1) * span)
        q_s[part, :] = q_ref[:, part]
        q_t[:, part] = q_ref[:, part].T
        go_s[part, :] = go_ref[:, part]
        turned = go_ref[:, part].T
        go_t[:, part] = turned
        delta[:, part] = jnp.sum(
            att_t_ref[0, 0, :, part].astype(F32) * turned.astype(F32), axis=0, keepdims=True
        )
    gq_t[...] = jnp.zeros_like(gq_t)

    def step(j, masked):
        start = pl.multiple_of(j * PAIR, PAIR)
        rows = pl.ds(start, PAIR)
        k_tile = k_sorted[rows, :]
        v_tile = v_sorted[rows, :]
        kt_tile = k_t[:, rows]
        parts = [slice(c, c + BACKWARD_COLS) for c in range(0, q_t.shape[1], BACKWARD_COLS)]
        ready, all_w, all_d = {}, [], []

        def multiply(n):
            ready[n] = (dot(k_tile, q_t[:, parts[n]]), dot(v_tile, go_t[:, parts[n]]))

        def weigh(n):
            cols = parts[n]
            products, dweights = ready.pop(n)
            scores = products * scale
            if masked:
                scores = mask_t(scores, start, query_block * span, span)
            weights = jnp.exp2(scores - lse_ref[0, 0, :, cols])
            all_w.append(weights.astype(BF16))
            all_d.append((weights * (dweights - delta[:, cols])).astype(BF16))

        def collect(n):
            gq_t[:, parts[n]] += dot(kt_tile, all_d[n])

        in_turn(len(parts), multiply, weigh, collect)
        gv[rows, :] += dot(jnp.concatenate(all_w, axis=1), go_s[...])
        gk[rows, :] += dot(jnp.concatenate(all_d, axis=1), q_s[...])

    last = query_block // 2
    pl.loop(0, last)(lambda j: step(j, False))
    step(last, True)

    for h in range(heads):
        part = slice(h * span, (h + 1) * span)
        gq_ref[:, part] = (gq_t[:, part] * out_scale).T.astype(BF16)

    @pl.when(half == 1)
    def _():
        for j in range(blocks):
            stored = info_ref[j]
            part = slice(j * span, (j + 1) * span)
            gkv_ref[stored // 2, 0, stored % 2] = (gk[part, :] * out_scale).astype(BF16)
            gkv_ref[stored // 2, 1, stored % 2] = gv[part, :].astype(BF16)


def project_kernel(info_ref, a_ref, w_ref, o_ref):
    o_ref[...] = dot(a_ref[...], w_ref[...]).astype(BF16)


def project(first, attended, weight, width):
    rows, depth = attended.shape
    tile = 1024
    return pl.pallas_call(
        project_kernel,
        out_shape=jax.ShapeDtypeStruct((rows, width), BF16),
        grid_spec=pltpu.PrefetchScalarGridSpec(
            num_scalar_prefetch=1,
            grid=(width // tile,),
            in_specs=[
                pl.BlockSpec((rows, depth), lambda i, info: (0, 0)),
                pl.BlockSpec((depth, tile), lambda i, info: (0, info[0] * (width // tile) + i)),
            ],
            out_specs=pl.BlockSpec((rows, tile), lambda i, info: (0, i)),
        ),
        compiler_params=pltpu.CompilerParams(vmem_limit_bytes=VMEM_LIMIT),
        cost_estimate=pl.CostEstimate(
            flops=2 * rows * depth * width, bytes_accessed=2 * depth * width, transcendentals=0
        ),
    )(first, attended, weight)


def forward(info, q2, kv_all, span):
    rows, flat = q2.shape
    ctx, kv2, _, _, hd = kv_all.shape
    kvl = kv2 // 2
    blocks = ctx * 2
    seq = blocks * span
    width = flat // kvl
    kernel = functools.partial(forward_kernel, blocks, span, LOG2E / math.sqrt(hd))
    work = rows * seq * flat // 2
    return pl.pallas_call(
        kernel,
        out_shape=(
            jax.ShapeDtypeStruct((rows, flat), BF16),
            jax.ShapeDtypeStruct((kvl, 2, hd, width), BF16),
            jax.ShapeDtypeStruct((kvl, 2, 1, width), F32),
        ),
        grid_spec=pltpu.PrefetchScalarGridSpec(
            num_scalar_prefetch=1,
            grid=(kvl, 2),
            in_specs=[
                pl.BlockSpec((span, width), lambda g, i, info: (i, g)),
                pl.BlockSpec((ctx, 1, 2, span, hd), lambda g, i, info: (0, g, 0, 0, 0)),
                pl.BlockSpec((ctx, 1, 2, span, hd), lambda g, i, info: (0, kvl + g, 0, 0, 0)),
            ],
            out_specs=(
                pl.BlockSpec((span, width), lambda g, i, info: (i, g)),
                pl.BlockSpec((1, 1, hd, width), lambda g, i, info: (g, i, 0, 0)),
                pl.BlockSpec((1, 1, 1, width), lambda g, i, info: (g, i, 0, 0)),
            ),
            scratch_shapes=[
                pltpu.VMEM((seq, hd), BF16),
                pltpu.VMEM((hd, seq), BF16),
                pltpu.VMEM((hd, width), BF16),
                pltpu.VMEM((hd, width), F32),
                pltpu.VMEM((1, width), F32),
                pltpu.VMEM((1, width), F32),
            ],
        ),
        compiler_params=pltpu.CompilerParams(vmem_limit_bytes=VMEM_LIMIT),
        cost_estimate=pl.CostEstimate(
            flops=8 * work, bytes_accessed=4 * rows * flat, transcendentals=work // hd
        ),
    )(info, q2, kv_all, kv_all)


def backward(info, q2, go2, kv_all, att_t, lse, span, g):
    rows, flat = q2.shape
    ctx, kv2, _, _, hd = kv_all.shape
    kvl = kv2 // 2
    blocks = ctx * 2
    seq = blocks * span
    width = flat // kvl
    kernel = functools.partial(
        backward_kernel, blocks, span, LOG2E / math.sqrt(hd), 1.0 / math.sqrt(hd)
    )
    work = rows * seq * width // 2
    return pl.pallas_call(
        kernel,
        out_shape=(
            jax.ShapeDtypeStruct((rows, width), BF16),
            jax.ShapeDtypeStruct((ctx, 2, 2, span, hd), BF16),
        ),
        grid_spec=pltpu.PrefetchScalarGridSpec(
            num_scalar_prefetch=1,
            grid=(2,),
            in_specs=[
                pl.BlockSpec((span, width), lambda i, info: (i, g)),
                pl.BlockSpec((span, width), lambda i, info: (i, g)),
                pl.BlockSpec((ctx, 1, 2, span, hd), lambda i, info: (0, g, 0, 0, 0)),
                pl.BlockSpec((ctx, 1, 2, span, hd), lambda i, info: (0, kvl + g, 0, 0, 0)),
                pl.BlockSpec((1, 1, hd, width), lambda i, info: (g, i, 0, 0)),
                pl.BlockSpec((1, 1, 1, width), lambda i, info: (g, i, 0, 0)),
            ],
            out_specs=(
                pl.BlockSpec((span, width), lambda i, info: (i, 0)),
                pl.BlockSpec((ctx, 2, 2, span, hd), lambda i, info: (0, 0, 0, 0, 0)),
            ),
            scratch_shapes=[
                pltpu.VMEM((seq, hd), BF16),
                pltpu.VMEM((seq, hd), BF16),
                pltpu.VMEM((hd, seq), BF16),
                pltpu.VMEM((width, hd), BF16),
                pltpu.VMEM((hd, width), BF16),
                pltpu.VMEM((width, hd), BF16),
                pltpu.VMEM((hd, width), BF16),
                pltpu.VMEM((hd, width), F32),
                pltpu.VMEM((1, width), F32),
                pltpu.VMEM((seq, hd), F32),
                pltpu.VMEM((seq, hd), F32),
            ],
        ),
        compiler_params=pltpu.CompilerParams(vmem_limit_bytes=VMEM_LIMIT),
        cost_estimate=pl.CostEstimate(
            flops=20 * work, bytes_accessed=4 * rows * flat, transcendentals=work // hd
        ),
    )(info, q2, go2, kv_all, kv_all, att_t, lse)


def local(queries, keys, values, positions, out_weight, grad_out):
    rows, heads, hd = queries.shape
    kvl = keys.shape[1]
    span = rows // 2
    ctx = lax.axis_size("ctx")
    tp = lax.axis_size("tp")
    me = lax.axis_index("tp")
    seq = rows * ctx
    blocks = 2 * ctx
    model = out_weight.shape[1]
    chunk = model // tp

    kv = jnp.stack([keys, values]).transpose(0, 2, 1, 3).reshape(2 * kvl, 2, span, hd)
    kv_all = lax.all_gather(kv, "ctx", axis=0, tiled=False)

    block_of = positions.reshape(blocks, span)[:, 0] // span
    order = jnp.arange(blocks, dtype=jnp.int32)
    place = jnp.sum(jnp.where(block_of[None, :] == order[:, None], order[None, :], 0), axis=1)
    mine = lax.dynamic_slice_in_dim(block_of, 2 * lax.axis_index("ctx"), 2)
    info = jnp.concatenate([place, mine]).astype(jnp.int32)

    q2 = queries.reshape(rows, heads * hd)
    grad_heads = lax.dot_general(
        grad_out, out_weight, (((1,), (1,)), ((), ())), preferred_element_type=F32
    ).astype(BF16)

    q2, grad_heads = lax.optimization_barrier((q2, grad_heads))
    attended, att_t, lse = forward(info, q2, kv_all, span)

    early = jnp.where(me < (tp + 1) // 2, tp - 1, 0).astype(jnp.int32).reshape(1)
    first = project(early, attended, out_weight, chunk)
    first, rest = lax.optimization_barrier((first, attended))
    partial_out = project(jnp.zeros((1,), jnp.int32), rest, out_weight, model)

    def own_part(index):
        index = jnp.clip(index, 0, tp - 1)
        return lax.dynamic_slice_in_dim(partial_out, index * chunk, chunk, axis=1)

    query_parts, kv_parts = [], []

    def key_value_sum(now):
        g = len(query_parts)
        gq, gkv = backward(info, now, grad_heads, kv_all, att_t, lse, span, g)
        query_parts.append(gq)
        terms = gkv.reshape(ctx, 2, rows, hd)
        kv_parts.append(lax.psum_scatter(terms, "ctx", scatter_dimension=0, tiled=False))

    right = left = first
    for k in range(tp - 1):
        to_right = [(z, z + 1) for z in range(tp - 1) if z <= k]
        to_left = [(tp - 1 - a, tp - 1 - b) for a, b in to_right]
        from_left = lax.ppermute(right, "tp", to_right).astype(F32)
        from_right = lax.ppermute(left, "tp", to_left).astype(F32)
        if k < tp - 2:
            right = (own_part(tp - 2 - k + me).astype(F32) + from_left).astype(BF16)
            left = (own_part(k + 2 - tp + me).astype(F32) + from_right).astype(BF16)
            right, left, q2 = lax.optimization_barrier((right, left, q2))
            if len(query_parts) < kvl:
                key_value_sum(q2)
    while len(query_parts) < kvl:
        key_value_sum(q2)
    layer_out = (own_part(me).astype(F32) + from_left + from_right).astype(BF16)

    grad_queries = jnp.concatenate(query_parts, axis=1).reshape(rows, heads, hd)
    owned = jnp.stack(kv_parts, axis=2)
    return (layer_out, grad_queries, owned[0], owned[1])


def solution(mesh):
    placed = (
        P("ctx", "tp", None),
        P("ctx", "tp", None),
        P("ctx", "tp", None),
        P(),
        P("tp", None),
        P("ctx", None),
    )
    return jax.shard_map(
        local,
        mesh=mesh,
        in_specs=placed,
        out_specs=(
            P("ctx", "tp"),
            P("ctx", "tp", None),
            P("ctx", "tp", None),
            P("ctx", "tp", None),
        ),
        check_vma=False,
    )
```

```python
import functools
import math

import jax
import jax.numpy as jnp
from jax import lax
from jax.experimental import pallas as pl
from jax.experimental.pallas import tpu as pltpu
from jax.sharding import PartitionSpec as P

NEG_FILL = -1e30
LOG2E = 1.4426950408889634
PAIR = 256
FORWARD_COLS = 512
BACKWARD_COLS = 256
F32 = jnp.float32
BF16 = jnp.bfloat16
VMEM_LIMIT = 50 * 1024 * 1024


def dot(a, b):
    return jnp.dot(a, b, preferred_element_type=F32)


def mask_t(scores, key_start, query_start, span):
    key_pos = key_start + lax.broadcasted_iota(jnp.int32, scores.shape, 0)
    query_pos = query_start + lax.broadcasted_iota(jnp.int32, scores.shape, 1) % span
    return jnp.where(key_pos <= query_pos, scores, NEG_FILL)


def in_turn(count, multiply, weigh, collect):
    for n in range(count + 2):
        if n < count:
            multiply(n)
        if 1 <= n <= count:
            weigh(n - 1)
        if n >= 2:
            collect(n - 2)


def load_sorted(info_ref, src_ref, blocks, span):
    for j in range(blocks):
        stored = info_ref[j]
        yield j, src_ref[stored // 2, 0, stored % 2]


def forward_kernel(blocks, span, scale, info_ref, q_ref, k_ref, v_ref, att_ref, att_t_ref, lse_ref,
                   k_sorted, v_t, q_t, out_t, top, total):
    half = pl.program_id(1)
    heads = q_ref.shape[1] // span
    query_block = info_ref[blocks + half]

    @pl.when(half == 0)
    def _():
        for j, block in load_sorted(info_ref, k_ref, blocks, span):
            k_sorted[j * span:(j + 1) * span, :] = block
        for j, block in load_sorted(info_ref, v_ref, blocks, span):
            v_t[:, j * span:(j + 1) * span] = block.T

    for h in range(heads):
        q_t[:, h * span:(h + 1) * span] = q_ref[:, h * span:(h + 1) * span].T
    out_t[...] = jnp.zeros_like(out_t)
    top[...] = jnp.full_like(top, NEG_FILL)
    total[...] = jnp.zeros_like(total)

    def step(j, masked):
        start = pl.multiple_of(j * PAIR, PAIR)
        k_tile = k_sorted[pl.ds(start, PAIR), :]
        v_tile = v_t[:, pl.ds(start, PAIR)]
        parts = [slice(c, c + FORWARD_COLS) for c in range(0, q_t.shape[1], FORWARD_COLS)]
        ready, weighted = {}, {}

        def multiply(n):
            ready[n] = dot(k_tile, q_t[:, parts[n]])

        def weigh(n):
            cols = parts[n]
            scores = ready.pop(n) * scale
            if masked:
                scores = mask_t(scores, start, query_block * span, span)
            old_top = top[:, cols]
            new_top = jnp.maximum(old_top, jnp.max(scores, axis=0, keepdims=True))
            weights = jnp.exp2(scores - new_top)
            factor = jnp.exp2(old_top - new_top)
            top[:, cols] = new_top
            total[:, cols] = total[:, cols] * factor + jnp.sum(weights, axis=0, keepdims=True)
            weighted[n] = (weights.astype(BF16), factor)

        def collect(n):
            weights, factor = weighted.pop(n)
            out_t[:, parts[n]] = out_t[:, parts[n]] * factor + dot(v_tile, weights)

        in_turn(len(parts), multiply, weigh, collect)

    last = query_block // 2
    pl.loop(0, last)(lambda j: step(j, False))
    step(last, True)

    lse_ref[0, 0] = top[...] + jnp.log2(total[...])
    inverse = 1.0 / total[...]
    for h in range(heads):
        cols = slice(h * span, (h + 1) * span)
        part = out_t[:, cols] * inverse[:, cols]
        att_t_ref[0, 0, :, cols] = part.astype(BF16)
        att_ref[:, cols] = part.T.astype(BF16)


def backward_kernel(blocks, span, scale, out_scale, info_ref, q_ref, go_ref, k_ref, v_ref, att_t_ref,
                    lse_ref, gq_ref, gkv_ref, k_sorted, v_sorted, k_t, q_s, q_t, go_s, go_t, gq_t,
                    delta, gk, gv):
    half = pl.program_id(0)
    heads = q_ref.shape[1] // span
    query_block = info_ref[blocks + half]

    @pl.when(half == 0)
    def _():
        for j, block in load_sorted(info_ref, k_ref, blocks, span):
            k_sorted[j * span:(j + 1) * span, :] = block
            k_t[:, j * span:(j + 1) * span] = block.T
        for j, block in load_sorted(info_ref, v_ref, blocks, span):
            v_sorted[j * span:(j + 1) * span, :] = block
        gk[...] = jnp.zeros_like(gk)
        gv[...] = jnp.zeros_like(gv)

    for h in range(heads):
        part = slice(h * span, (h + 1) * span)
        q_s[part, :] = q_ref[:, part]
        q_t[:, part] = q_ref[:, part].T
        go_s[part, :] = go_ref[:, part]
        turned = go_ref[:, part].T
        go_t[:, part] = turned
        delta[:, part] = jnp.sum(
            att_t_ref[0, 0, :, part].astype(F32) * turned.astype(F32), axis=0, keepdims=True
        )
    gq_t[...] = jnp.zeros_like(gq_t)

    def step(j, masked):
        start = pl.multiple_of(j * PAIR, PAIR)
        rows = pl.ds(start, PAIR)
        k_tile = k_sorted[rows, :]
        v_tile = v_sorted[rows, :]
        kt_tile = k_t[:, rows]
        parts = [slice(c, c + BACKWARD_COLS) for c in range(0, q_t.shape[1], BACKWARD_COLS)]
        ready, all_w, all_d = {}, [], []

        def multiply(n):
            ready[n] = (dot(k_tile, q_t[:, parts[n]]), dot(v_tile, go_t[:, parts[n]]))

        def weigh(n):
            cols = parts[n]
            products, dweights = ready.pop(n)
            scores = products * scale
            if masked:
                scores = mask_t(scores, start, query_block * span, span)
            weights = jnp.exp2(scores - lse_ref[0, 0, :, cols])
            all_w.append(weights.astype(BF16))
            all_d.append((weights * (dweights - delta[:, cols])).astype(BF16))

        def collect(n):
            gq_t[:, parts[n]] += dot(kt_tile, all_d[n])

        in_turn(len(parts), multiply, weigh, collect)
        gv[rows, :] += dot(jnp.concatenate(all_w, axis=1), go_s[...])
        gk[rows, :] += dot(jnp.concatenate(all_d, axis=1), q_s[...])

    last = query_block // 2
    pl.loop(0, last)(lambda j: step(j, False))
    step(last, True)

    for h in range(heads):
        part = slice(h * span, (h + 1) * span)
        gq_ref[:, part] = (gq_t[:, part] * out_scale).T.astype(BF16)

    @pl.when(half == 1)
    def _():
        for j in range(blocks):
            stored = info_ref[j]
            part = slice(j * span, (j + 1) * span)
            gkv_ref[stored // 2, 0, stored % 2] = (gk[part, :] * out_scale).astype(BF16)
            gkv_ref[stored // 2, 1, stored % 2] = gv[part, :].astype(BF16)


def project_kernel(info_ref, a_ref, w_ref, o_ref):
    o_ref[...] = dot(a_ref[...], w_ref[...]).astype(BF16)


def project(first, attended, weight, width):
    rows, depth = attended.shape
    tile = 1024
    return pl.pallas_call(
        project_kernel,
        out_shape=jax.ShapeDtypeStruct((rows, width), BF16),
        grid_spec=pltpu.PrefetchScalarGridSpec(
            num_scalar_prefetch=1,
            grid=(width // tile,),
            in_specs=[
                pl.BlockSpec((rows, depth), lambda i, info: (0, 0)),
                pl.BlockSpec((depth, tile), lambda i, info: (0, info[0] * (width // tile) + i)),
            ],
            out_specs=pl.BlockSpec((rows, tile), lambda i, info: (0, i)),
        ),
        compiler_params=pltpu.CompilerParams(vmem_limit_bytes=VMEM_LIMIT),
        cost_estimate=pl.CostEstimate(
            flops=2 * rows * depth * width, bytes_accessed=2 * depth * width, transcendentals=0
        ),
    )(first, attended, weight)


def forward(info, q2, kv_all, span):
    rows, flat = q2.shape
    ctx, kv2, _, _, hd = kv_all.shape
    kvl = kv2 // 2
    blocks = ctx * 2
    seq = blocks * span
    width = flat // kvl
    kernel = functools.partial(forward_kernel, blocks, span, LOG2E / math.sqrt(hd))
    work = rows * seq * flat // 2
    return pl.pallas_call(
        kernel,
        out_shape=(
            jax.ShapeDtypeStruct((rows, flat), BF16),
            jax.ShapeDtypeStruct((kvl, 2, hd, width), BF16),
            jax.ShapeDtypeStruct((kvl, 2, 1, width), F32),
        ),
        grid_spec=pltpu.PrefetchScalarGridSpec(
            num_scalar_prefetch=1,
            grid=(kvl, 2),
            in_specs=[
                pl.BlockSpec((span, width), lambda g, i, info: (i, g)),
                pl.BlockSpec((ctx, 1, 2, span, hd), lambda g, i, info: (0, g, 0, 0, 0)),
                pl.BlockSpec((ctx, 1, 2, span, hd), lambda g, i, info: (0, kvl + g, 0, 0, 0)),
            ],
            out_specs=(
                pl.BlockSpec((span, width), lambda g, i, info: (i, g)),
                pl.BlockSpec((1, 1, hd, width), lambda g, i, info: (g, i, 0, 0)),
                pl.BlockSpec((1, 1, 1, width), lambda g, i, info: (g, i, 0, 0)),
            ),
            scratch_shapes=[
                pltpu.VMEM((seq, hd), BF16),
                pltpu.VMEM((hd, seq), BF16),
                pltpu.VMEM((hd, width), BF16),
                pltpu.VMEM((hd, width), F32),
                pltpu.VMEM((1, width), F32),
                pltpu.VMEM((1, width), F32),
            ],
        ),
        compiler_params=pltpu.CompilerParams(vmem_limit_bytes=VMEM_LIMIT),
        cost_estimate=pl.CostEstimate(
            flops=8 * work, bytes_accessed=4 * rows * flat, transcendentals=work // hd
        ),
    )(info, q2, kv_all, kv_all)


def backward(info, q2, go2, kv_all, att_t, lse, span, g):
    rows, flat = q2.shape
    ctx, kv2, _, _, hd = kv_all.shape
    kvl = kv2 // 2
    blocks = ctx * 2
    seq = blocks * span
    width = flat // kvl
    kernel = functools.partial(
        backward_kernel, blocks, span, LOG2E / math.sqrt(hd), 1.0 / math.sqrt(hd)
    )
    work = rows * seq * width // 2
    return pl.pallas_call(
        kernel,
        out_shape=(
            jax.ShapeDtypeStruct((rows, width), BF16),
            jax.ShapeDtypeStruct((ctx, 2, 2, span, hd), BF16),
        ),
        grid_spec=pltpu.PrefetchScalarGridSpec(
            num_scalar_prefetch=1,
            grid=(2,),
            in_specs=[
                pl.BlockSpec((span, width), lambda i, info: (i, g)),
                pl.BlockSpec((span, width), lambda i, info: (i, g)),
                pl.BlockSpec((ctx, 1, 2, span, hd), lambda i, info: (0, g, 0, 0, 0)),
                pl.BlockSpec((ctx, 1, 2, span, hd), lambda i, info: (0, kvl + g, 0, 0, 0)),
                pl.BlockSpec((1, 1, hd, width), lambda i, info: (g, i, 0, 0)),
                pl.BlockSpec((1, 1, 1, width), lambda i, info: (g, i, 0, 0)),
            ],
            out_specs=(
                pl.BlockSpec((span, width), lambda i, info: (i, 0)),
                pl.BlockSpec((ctx, 2, 2, span, hd), lambda i, info: (0, 0, 0, 0, 0)),
            ),
            scratch_shapes=[
                pltpu.VMEM((seq, hd), BF16),
                pltpu.VMEM((seq, hd), BF16),
                pltpu.VMEM((hd, seq), BF16),
                pltpu.VMEM((width, hd), BF16),
                pltpu.VMEM((hd, width), BF16),
                pltpu.VMEM((width, hd), BF16),
                pltpu.VMEM((hd, width), BF16),
                pltpu.VMEM((hd, width), F32),
                pltpu.VMEM((1, width), F32),
                pltpu.VMEM((seq, hd), F32),
                pltpu.VMEM((seq, hd), F32),
            ],
        ),
        compiler_params=pltpu.CompilerParams(vmem_limit_bytes=VMEM_LIMIT),
        cost_estimate=pl.CostEstimate(
            flops=20 * work, bytes_accessed=4 * rows * flat, transcendentals=work // hd
        ),
    )(info, q2, go2, kv_all, kv_all, att_t, lse)


def local(queries, keys, values, positions, out_weight, grad_out):
    rows, heads, hd = queries.shape
    kvl = keys.shape[1]
    span = rows // 2
    ctx = lax.axis_size("ctx")
    tp = lax.axis_size("tp")
    me = lax.axis_index("tp")
    seq = rows * ctx
    blocks = 2 * ctx
    model = out_weight.shape[1]
    chunk = model // tp

    kv = jnp.stack([keys, values]).transpose(0, 2, 1, 3).reshape(2 * kvl, 2, span, hd)
    kv_all = lax.all_gather(kv, "ctx", axis=0, tiled=False)

    block_of = positions.reshape(blocks, span)[:, 0] // span
    order = jnp.arange(blocks, dtype=jnp.int32)
    place = jnp.sum(jnp.where(block_of[None, :] == order[:, None], order[None, :], 0), axis=1)
    mine = lax.dynamic_slice_in_dim(block_of, 2 * lax.axis_index("ctx"), 2)
    info = jnp.concatenate([place, mine]).astype(jnp.int32)

    q2 = queries.reshape(rows, heads * hd)
    grad_heads = lax.dot_general(
        grad_out, out_weight, (((1,), (1,)), ((), ())), preferred_element_type=F32
    ).astype(BF16)

    q2, grad_heads = lax.optimization_barrier((q2, grad_heads))
    attended, att_t, lse = forward(info, q2, kv_all, span)

    early = jnp.where(me < (tp + 1) // 2, tp - 1, 0).astype(jnp.int32).reshape(1)
    first = project(early, attended, out_weight, chunk)
    first, rest = lax.optimization_barrier((first, attended))
    partial_out = project(jnp.zeros((1,), jnp.int32), rest, out_weight, model)

    def own_part(index):
        index = jnp.clip(index, 0, tp - 1)
        return lax.dynamic_slice_in_dim(partial_out, index * chunk, chunk, axis=1)

    def gradients(now):
        parts = [backward(info, now, grad_heads, kv_all, att_t, lse, span, g) for g in range(kvl)]
        queries_part = jnp.concatenate([part[0] for part in parts], axis=1)
        terms = jnp.stack([part[1] for part in parts], axis=1).reshape(ctx, kvl, 2, rows, hd)
        return queries_part, lax.psum_scatter(terms, "ctx", scatter_dimension=0, tiled=False)

    grads = None
    right = left = first
    for k in range(tp - 1):
        to_right = [(z, z + 1) for z in range(tp - 1) if z <= k]
        to_left = [(tp - 1 - a, tp - 1 - b) for a, b in to_right]
        from_left = lax.ppermute(right, "tp", to_right).astype(F32)
        from_right = lax.ppermute(left, "tp", to_left).astype(F32)
        if k < tp - 2:
            right = (own_part(tp - 2 - k + me).astype(F32) + from_left).astype(BF16)
            left = (own_part(k + 2 - tp + me).astype(F32) + from_right).astype(BF16)
            right, left, q2 = lax.optimization_barrier((right, left, q2))
            if grads is None:
                grads = gradients(q2)
    if grads is None:
        grads = gradients(q2)
    layer_out = (own_part(me).astype(F32) + from_left + from_right).astype(BF16)

    grad_queries = grads[0].reshape(rows, heads, hd)
    owned = grads[1].transpose(1, 2, 0, 3)
    return (layer_out, grad_queries, owned[0], owned[1])


def solution(mesh):
    placed = (
        P("ctx", "tp", None),
        P("ctx", "tp", None),
        P("ctx", "tp", None),
        P(),
        P("tp", None),
        P("ctx", None),
    )
    return jax.shard_map(
        local,
        mesh=mesh,
        in_specs=placed,
        out_specs=(
            P("ctx", "tp"),
            P("ctx", "tp", None),
            P("ctx", "tp", None),
            P("ctx", "tp", None),
        ),
        check_vma=False,
    )
```

```python
import functools
import math

import jax
import jax.numpy as jnp
from jax import lax
from jax.experimental import pallas as pl
from jax.experimental.pallas import tpu as pltpu
from jax.sharding import PartitionSpec as P

NEG_FILL = -1e30
LOG2E = 1.4426950408889634
PAIR = 256
FORWARD_COLS = 512
BACKWARD_COLS = 256
F32 = jnp.float32
BF16 = jnp.bfloat16
VMEM_LIMIT = 50 * 1024 * 1024


def dot(a, b):
    return jnp.dot(a, b, preferred_element_type=F32)


def mask_t(scores, key_start, query_start, span):
    key_pos = key_start + lax.broadcasted_iota(jnp.int32, scores.shape, 0)
    query_pos = query_start + lax.broadcasted_iota(jnp.int32, scores.shape, 1) % span
    return jnp.where(key_pos <= query_pos, scores, NEG_FILL)


def in_turn(count, multiply, weigh, collect):
    for n in range(count + 2):
        if n < count:
            multiply(n)
        if 1 <= n <= count:
            weigh(n - 1)
        if n >= 2:
            collect(n - 2)


def load_sorted(info_ref, src_ref, blocks, span):
    for j in range(blocks):
        stored = info_ref[j]
        yield j, src_ref[stored // 2, 0, stored % 2]


def forward_kernel(blocks, span, scale, info_ref, q_ref, k_ref, v_ref, att_ref, att_t_ref, lse_ref,
                   k_sorted, v_t, q_t, out_t, top, total):
    half = pl.program_id(1)
    heads = q_ref.shape[1] // span
    query_block = info_ref[blocks + half]

    @pl.when(half == 0)
    def _():
        for j, block in load_sorted(info_ref, k_ref, blocks, span):
            k_sorted[j * span:(j + 1) * span, :] = block
        for j, block in load_sorted(info_ref, v_ref, blocks, span):
            v_t[:, j * span:(j + 1) * span] = block.T

    for h in range(heads):
        q_t[:, h * span:(h + 1) * span] = q_ref[:, h * span:(h + 1) * span].T
    out_t[...] = jnp.zeros_like(out_t)
    top[...] = jnp.full_like(top, NEG_FILL)
    total[...] = jnp.zeros_like(total)

    def step(j, masked):
        start = pl.multiple_of(j * PAIR, PAIR)
        k_tile = k_sorted[pl.ds(start, PAIR), :]
        v_tile = v_t[:, pl.ds(start, PAIR)]
        parts = [slice(c, c + FORWARD_COLS) for c in range(0, q_t.shape[1], FORWARD_COLS)]
        ready, weighted = {}, {}

        def multiply(n):
            ready[n] = dot(k_tile, q_t[:, parts[n]])

        def weigh(n):
            cols = parts[n]
            scores = ready.pop(n) * scale
            if masked:
                scores = mask_t(scores, start, query_block * span, span)
            old_top = top[:, cols]
            new_top = jnp.maximum(old_top, jnp.max(scores, axis=0, keepdims=True))
            weights = jnp.exp2(scores - new_top)
            factor = jnp.exp2(old_top - new_top)
            top[:, cols] = new_top
            total[:, cols] = total[:, cols] * factor + jnp.sum(weights, axis=0, keepdims=True)
            weighted[n] = (weights.astype(BF16), factor)

        def collect(n):
            weights, factor = weighted.pop(n)
            out_t[:, parts[n]] = out_t[:, parts[n]] * factor + dot(v_tile, weights)

        in_turn(len(parts), multiply, weigh, collect)

    last = query_block // 2
    pl.loop(0, last)(lambda j: step(j, False))
    step(last, True)

    lse_ref[0, 0] = top[...] + jnp.log2(total[...])
    inverse = 1.0 / total[...]
    for h in range(heads):
        cols = slice(h * span, (h + 1) * span)
        part = (out_t[:, cols] * inverse[:, cols]).astype(BF16)
        att_t_ref[0, 0, :, cols] = part
        att_ref[:, cols] = part.T


def backward_kernel(blocks, span, scale, out_scale, info_ref, q_ref, go_ref, k_ref, v_ref, att_t_ref,
                    lse_ref, gq_ref, gkv_ref, k_sorted, v_sorted, k_t, q_s, q_t, go_s, go_t, gq_t,
                    delta, gk, gv):
    half = pl.program_id(1)
    heads = q_ref.shape[1] // span
    query_block = info_ref[blocks + half]

    @pl.when(half == 0)
    def _():
        for j, block in load_sorted(info_ref, k_ref, blocks, span):
            k_sorted[j * span:(j + 1) * span, :] = block
            k_t[:, j * span:(j + 1) * span] = block.T
        for j, block in load_sorted(info_ref, v_ref, blocks, span):
            v_sorted[j * span:(j + 1) * span, :] = block
        gk[...] = jnp.zeros_like(gk)
        gv[...] = jnp.zeros_like(gv)

    for h in range(heads):
        part = slice(h * span, (h + 1) * span)
        q_s[part, :] = q_ref[:, part]
        q_t[:, part] = q_ref[:, part].T
        go_s[part, :] = go_ref[:, part]
        turned = go_ref[:, part].T
        go_t[:, part] = turned
        delta[:, part] = jnp.sum(
            att_t_ref[0, 0, :, part].astype(F32) * turned.astype(F32), axis=0, keepdims=True
        )
    gq_t[...] = jnp.zeros_like(gq_t)

    def step(j, masked):
        start = pl.multiple_of(j * PAIR, PAIR)
        rows = pl.ds(start, PAIR)
        k_tile = k_sorted[rows, :]
        v_tile = v_sorted[rows, :]
        kt_tile = k_t[:, rows]
        parts = [slice(c, c + BACKWARD_COLS) for c in range(0, q_t.shape[1], BACKWARD_COLS)]
        ready, all_w, all_d = {}, [], []

        def multiply(n):
            ready[n] = (dot(k_tile, q_t[:, parts[n]]), dot(v_tile, go_t[:, parts[n]]))

        def weigh(n):
            cols = parts[n]
            products, dweights = ready.pop(n)
            scores = products * scale
            if masked:
                scores = mask_t(scores, start, query_block * span, span)
            weights = jnp.exp2(scores - lse_ref[0, 0, :, cols])
            all_w.append(weights.astype(BF16))
            all_d.append((weights * (dweights - delta[:, cols])).astype(BF16))

        def collect(n):
            gq_t[:, parts[n]] += dot(kt_tile, all_d[n])

        in_turn(len(parts), multiply, weigh, collect)
        gv[rows, :] += dot(jnp.concatenate(all_w, axis=1), go_s[...])
        gk[rows, :] += dot(jnp.concatenate(all_d, axis=1), q_s[...])

    last = query_block // 2
    pl.loop(0, last)(lambda j: step(j, False))
    step(last, True)

    for h in range(heads):
        part = slice(h * span, (h + 1) * span)
        gq_ref[:, part] = (gq_t[:, part] * out_scale).astype(BF16).T

    @pl.when(half == 1)
    def _():
        for j in range(blocks):
            stored = info_ref[j]
            part = slice(j * span, (j + 1) * span)
            gkv_ref[stored // 2, 0, 0, stored % 2] = (gk[part, :] * out_scale).astype(BF16)
            gkv_ref[stored // 2, 0, 1, stored % 2] = gv[part, :].astype(BF16)


def project_kernel(info_ref, a_ref, w_ref, o_ref):
    o_ref[...] = dot(a_ref[...], w_ref[...]).astype(BF16)


def project(first, attended, weight, width):
    rows, depth = attended.shape
    tile = min(1024, width)
    return pl.pallas_call(
        project_kernel,
        out_shape=jax.ShapeDtypeStruct((rows, width), BF16),
        grid_spec=pltpu.PrefetchScalarGridSpec(
            num_scalar_prefetch=1,
            grid=(width // tile,),
            in_specs=[
                pl.BlockSpec((rows, depth), lambda i, info: (0, 0)),
                pl.BlockSpec((depth, tile), lambda i, info: (0, info[0] * (width // tile) + i)),
            ],
            out_specs=pl.BlockSpec((rows, tile), lambda i, info: (0, i)),
        ),
        compiler_params=pltpu.CompilerParams(vmem_limit_bytes=VMEM_LIMIT),
        cost_estimate=pl.CostEstimate(
            flops=2 * rows * depth * width, bytes_accessed=2 * depth * width, transcendentals=0
        ),
    )(first, attended, weight)


def forward(info, q2, kv_all, span):
    rows, flat = q2.shape
    ctx, kv2, _, _, hd = kv_all.shape
    kvl = kv2 // 2
    blocks = ctx * 2
    seq = blocks * span
    width = flat // kvl
    kernel = functools.partial(forward_kernel, blocks, span, LOG2E / math.sqrt(hd))
    work = rows * seq * flat // 2
    return pl.pallas_call(
        kernel,
        out_shape=(
            jax.ShapeDtypeStruct((rows, flat), BF16),
            jax.ShapeDtypeStruct((kvl, 2, hd, width), BF16),
            jax.ShapeDtypeStruct((kvl, 2, 1, width), F32),
        ),
        grid_spec=pltpu.PrefetchScalarGridSpec(
            num_scalar_prefetch=1,
            grid=(kvl, 2),
            in_specs=[
                pl.BlockSpec((span, width), lambda g, i, info: (i, g)),
                pl.BlockSpec((ctx, 1, 2, span, hd), lambda g, i, info: (0, g, 0, 0, 0)),
                pl.BlockSpec((ctx, 1, 2, span, hd), lambda g, i, info: (0, kvl + g, 0, 0, 0)),
            ],
            out_specs=(
                pl.BlockSpec((span, width), lambda g, i, info: (i, g)),
                pl.BlockSpec((1, 1, hd, width), lambda g, i, info: (g, i, 0, 0)),
                pl.BlockSpec((1, 1, 1, width), lambda g, i, info: (g, i, 0, 0)),
            ),
            scratch_shapes=[
                pltpu.VMEM((seq, hd), BF16),
                pltpu.VMEM((hd, seq), BF16),
                pltpu.VMEM((hd, width), BF16),
                pltpu.VMEM((hd, width), F32),
                pltpu.VMEM((1, width), F32),
                pltpu.VMEM((1, width), F32),
            ],
        ),
        compiler_params=pltpu.CompilerParams(vmem_limit_bytes=VMEM_LIMIT),
        cost_estimate=pl.CostEstimate(
            flops=8 * work, bytes_accessed=4 * rows * flat, transcendentals=work // hd
        ),
    )(info, q2, kv_all, kv_all)


def backward(info, q2, go2, kv_all, att_t, lse, span):
    rows, flat = q2.shape
    ctx, kv2, _, _, hd = kv_all.shape
    kvl = kv2 // 2
    blocks = ctx * 2
    seq = blocks * span
    width = flat // kvl
    kernel = functools.partial(
        backward_kernel, blocks, span, LOG2E / math.sqrt(hd), 1.0 / math.sqrt(hd)
    )
    work = rows * seq * flat // 2
    return pl.pallas_call(
        kernel,
        out_shape=(
            jax.ShapeDtypeStruct((rows, flat), BF16),
            jax.ShapeDtypeStruct((ctx, kvl, 2, 2, span, hd), BF16),
        ),
        grid_spec=pltpu.PrefetchScalarGridSpec(
            num_scalar_prefetch=1,
            grid=(kvl, 2),
            in_specs=[
                pl.BlockSpec((span, width), lambda g, i, info: (i, g)),
                pl.BlockSpec((span, width), lambda g, i, info: (i, g)),
                pl.BlockSpec((ctx, 1, 2, span, hd), lambda g, i, info: (0, g, 0, 0, 0)),
                pl.BlockSpec((ctx, 1, 2, span, hd), lambda g, i, info: (0, kvl + g, 0, 0, 0)),
                pl.BlockSpec((1, 1, hd, width), lambda g, i, info: (g, i, 0, 0)),
                pl.BlockSpec((1, 1, 1, width), lambda g, i, info: (g, i, 0, 0)),
            ],
            out_specs=(
                pl.BlockSpec((span, width), lambda g, i, info: (i, g)),
                pl.BlockSpec((ctx, 1, 2, 2, span, hd), lambda g, i, info: (0, g, 0, 0, 0, 0)),
            ),
            scratch_shapes=[
                pltpu.VMEM((seq, hd), BF16),
                pltpu.VMEM((seq, hd), BF16),
                pltpu.VMEM((hd, seq), BF16),
                pltpu.VMEM((width, hd), BF16),
                pltpu.VMEM((hd, width), BF16),
                pltpu.VMEM((width, hd), BF16),
                pltpu.VMEM((hd, width), BF16),
                pltpu.VMEM((hd, width), F32),
                pltpu.VMEM((1, width), F32),
                pltpu.VMEM((seq, hd), F32),
                pltpu.VMEM((seq, hd), F32),
            ],
        ),
        compiler_params=pltpu.CompilerParams(vmem_limit_bytes=VMEM_LIMIT),
        cost_estimate=pl.CostEstimate(
            flops=20 * work, bytes_accessed=4 * rows * flat, transcendentals=work // hd
        ),
    )(info, q2, go2, kv_all, kv_all, att_t, lse)


def local(queries, keys, values, positions, out_weight, grad_out):
    rows, heads, hd = queries.shape
    kvl = keys.shape[1]
    span = rows // 2
    ctx = lax.axis_size("ctx")
    tp = lax.axis_size("tp")
    me = lax.axis_index("tp")
    seq = rows * ctx
    blocks = 2 * ctx
    model = out_weight.shape[1]
    chunk = model // tp

    kv = jnp.stack([keys, values]).transpose(0, 2, 1, 3).reshape(2 * kvl, 2, span, hd)
    kv_all = lax.all_gather(kv, "ctx", axis=0, tiled=False)

    block_of = positions.reshape(blocks, span)[:, 0] // span
    order = jnp.arange(blocks, dtype=jnp.int32)
    place = jnp.sum(jnp.where(block_of[None, :] == order[:, None], order[None, :], 0), axis=1)
    mine = lax.dynamic_slice_in_dim(block_of, 2 * lax.axis_index("ctx"), 2)
    info = jnp.concatenate([place, mine]).astype(jnp.int32)

    q2 = queries.reshape(rows, heads * hd)
    grad_heads = lax.dot_general(
        grad_out, out_weight, (((1,), (1,)), ((), ())), preferred_element_type=F32
    ).astype(BF16)

    q2, grad_heads = lax.optimization_barrier((q2, grad_heads))
    attended, att_t, lse = forward(info, q2, kv_all, span)

    early = jnp.where(me < (tp + 1) // 2, tp - 1, 0).astype(jnp.int32).reshape(1)
    first = project(early, attended, out_weight, chunk)
    first, rest = lax.optimization_barrier((first, attended))
    partial_out = project(jnp.zeros((1,), jnp.int32), rest, out_weight, model)

    def own_part(index):
        index = jnp.clip(index, 0, tp - 1)
        return lax.dynamic_slice_in_dim(partial_out, index * chunk, chunk, axis=1)

    def gradients(now):
        queries_part, terms = backward(info, now, grad_heads, kv_all, att_t, lse, span)
        terms = terms.reshape(ctx, kvl, 2, rows, hd)
        return queries_part, lax.psum_scatter(terms, "ctx", scatter_dimension=0, tiled=False)

    grads = None
    right = left = first
    for k in range(tp - 1):
        to_right = [(z, z + 1) for z in range(tp - 1) if z <= k]
        to_left = [(tp - 1 - a, tp - 1 - b) for a, b in to_right]
        from_left = lax.ppermute(right, "tp", to_right).astype(F32)
        from_right = lax.ppermute(left, "tp", to_left).astype(F32)
        if k < tp - 2:
            right = (own_part(tp - 2 - k + me).astype(F32) + from_left).astype(BF16)
            left = (own_part(k + 2 - tp + me).astype(F32) + from_right).astype(BF16)
            right, left, q2 = lax.optimization_barrier((right, left, q2))
            if grads is None:
                grads = gradients(q2)
    if grads is None:
        grads = gradients(q2)
    layer_out = (own_part(me).astype(F32) + from_left + from_right).astype(BF16)

    grad_queries = grads[0].reshape(rows, heads, hd)
    owned = grads[1].transpose(1, 2, 0, 3)
    return (layer_out, grad_queries, owned[0], owned[1])


def solution(mesh):
    placed = (
        P("ctx", "tp", None),
        P("ctx", "tp", None),
        P("ctx", "tp", None),
        P(),
        P("tp", None),
        P("ctx", None),
    )
    return jax.shard_map(
        local,
        mesh=mesh,
        in_specs=placed,
        out_specs=(
            P("ctx", "tp"),
            P("ctx", "tp", None),
            P("ctx", "tp", None),
            P("ctx", "tp", None),
        ),
        check_vma=False,
    )
```
